32 devices in a mesh: dp: 2 (over core), expert: 16 (over z, y, x), tensor: 1.
Axes of the slice: x: 2, y: 2, z: 4, core: 2. Of those that a mesh axis runs over, the one named last changes fastest.
Arguments:
- tokens: bfloat16 [2048, 2048], P(('dp', 'expert'), 'tensor'), may hold values from -6 to 6
- expert_ids: int32 [2048, 6], P(('dp', 'expert')), may hold values from 0 to 15, all different within a row; in each aligned block of 64 rows (0 to 63, 64 to 127, ...) at most 32 rows name the same one
- route_weights: float32 [2048, 6], P(('dp', 'expert')), may hold values from 0.1 to 1
- w_gate: bfloat16 [16, 1408, 2048], P('expert', 'tensor'), may hold values from -0.125 to 0.125
- w_up: bfloat16 [16, 1408, 2048], P('expert', 'tensor'), may hold values from -0.125 to 0.125
- w_down: bfloat16 [16, 1408, 2048], P('expert', 'tensor'), may hold values from -0.15625 to 0.15625
- out_grad: bfloat16 [2048, 2048], P(('dp', 'expert'), 'tensor'), may hold values from -6 to 6
Outputs:
- layer_out: bfloat16 [2048, 2048], P(('dp', 'expert'), 'tensor')
- grad_tokens: bfloat16 [2048, 2048], P(('dp', 'expert'), 'tensor')
- grad_weights: float32 [2048, 6], P(('dp', 'expert'))
- grad_gate: bfloat16 [16, 1408, 2048], P('expert', 'tensor')
- grad_up: bfloat16 [16, 1408, 2048], P('expert', 'tensor')
- grad_down: bfloat16 [16, 1408, 2048], P('expert', 'tensor')
The draws below stay inside these ranges and needn't reach their ends.
Inputs may be any that keep to these rules, and one draw needn't show every extreme that they name: `expert_ids`: each row names 6 different experts. In each aligned block of 64 rows no expert is named more than 32 times, a bound that some block reaches.
All inputs are finite; a program needn't handle non-finite values.
Results may differ from the reference program's by a relative error of at most 0.014.
Values may be sent and summed in bfloat16 or wider, within the bound.
A program may use at most 128 MiB of HBM per device.

```python
import math
import jax
import jax.numpy as jnp
import numpy as np
from jax import lax

D = 2048
H = 1408
TOPK = 6
TOK_DEV = 64
EXPERTS = 16
CAP = 32
TOKENS = 2048
N_DP = 2
N_EXPERT = 16
N_TENSOR = 1


def block_levels(key, extent, pieces, smallest, high):
    level = 1.0
    for dim, blocks in pieces:
        steps = jax.random.uniform(jax.random.fold_in(jax.random.fold_in(key, 6), dim), (blocks,), jnp.float32, smallest / len(pieces), high / len(pieces))
        level = level * jnp.repeat(jnp.exp(steps), extent[dim] // blocks).reshape((-1,) + (1,) * (len(extent) - 1 - dim))
    return level


def deal_out(key, own, number, rows, count, top, reach, skew):
    ranking = jax.random.permutation(key, count)
    packed, ordinary = portions_of(count, rows * top, reach, skew, True), portions_of(count, rows * top, reach, skew, False)
    places = jnp.arange(count)

    def named(tallies, rotation):
        used = int((tallies > 0).sum())
        fixed = max(1, used // 4)
        passed = fixed + (places - fixed + rotation * (used - fixed)) % max(1, count - fixed)
        return jnp.zeros((count,), jnp.int32).at[ranking[jnp.where(places < fixed, places, passed)]].set(jnp.asarray(tallies, jnp.int32))

    tallies = jnp.where(number % 4 == 0, named(packed, number // 4), named(ordinary, number - number // 4 - 1))
    mixed = jax.random.permutation(jax.random.fold_in(own, 3), count)
    giver, receiver = mixed[0:count // 2 * 2:2], mixed[1:count // 2 * 2:2]
    room = jnp.minimum(tallies[giver] - 1, reach - tallies[receiver]) // 2
    room = jnp.where((giver == ranking[0]) | (receiver == ranking[0]) | (tallies[receiver] == 0), 0, jnp.maximum(room, 0))
    passed = jax.random.randint(jax.random.fold_in(own, 4), (count // 2,), 0, 1 << 20) % (room + 1)
    tallies = tallies.at[giver].add(-passed).at[receiver].add(passed)
    members = jnp.searchsorted(jnp.cumsum(tallies), jnp.arange(rows * top), side="right").astype(jnp.int32)
    grid = members.reshape(top, rows).T
    grid = grid[jax.random.permutation(jax.random.fold_in(own, 1), rows)]
    rotation = jax.random.randint(jax.random.fold_in(own, 2), (rows, 1), 0, top)
    return jnp.take_along_axis(grid, (jnp.arange(top)[None, :] + rotation) % top, axis=1)


def portions_of(amount, total, limit, skew, full):
    loads = [(1 << 20) // math.isqrt(standing ** skew) + 1 for standing in range(1, amount + 1)]
    largest = limit if full else min(limit, max(-(-total // amount), total * loads[0] // sum(loads)))
    least = 1 if total - largest >= amount - 1 else 0
    counts, rest = [largest] + [least] * (amount - 1), total - largest - least * (amount - 1)
    while rest > 0:
        movable = [i for i in range(1, amount) if counts[i] < largest] or [i for i in range(1, amount) if counts[i] < limit]
        pool, budget = sum([loads[i] for i in movable]), rest
        for i in movable:
            addition = min(limit - counts[i], max(1, budget * loads[i] // pool), rest)
            counts[i] = counts[i] + addition
            rest = rest - addition
    return np.array(counts)


def noise(stream_key, extent, spread, most, cuts=(), held_as=jnp.bfloat16):
    array = spread * jax.random.normal(stream_key, extent, jnp.float32)
    if cuts:
        array = array * block_levels(stream_key, extent, cuts, -0.22, 0.18)
    return jnp.clip(array, -most, most).astype(held_as)


def setup_inputs(seed: int = 0) -> dict:
    seeds = jax.random.split(jax.random.key(seed), 8)
    tokens = noise(seeds[0], (TOKENS, D), 1.0, 6.0, ((0, 32),))
    expert_ids_keys = jax.random.split(jax.random.fold_in(seeds[1], 1), TOKENS // TOK_DEV)
    expert_ids_turns = jax.random.permutation(jax.random.fold_in(seeds[1], 3), TOKENS // TOK_DEV)
    expert_ids = jax.vmap(lambda own, number: deal_out(jax.random.fold_in(seeds[1], 2), own, number, TOK_DEV, EXPERTS, TOPK, CAP, 2))(expert_ids_keys, expert_ids_turns).reshape((TOKENS, TOPK))
    route_weights = jnp.clip(jnp.exp(math.log(1.0) - 2.3025851 * jax.random.uniform(seeds[2], (TOKENS, TOPK), jnp.float32) ** block_levels(seeds[2], (TOKENS, TOPK), ((0, 32),), -0.2, 0.2)), 0.1, 1.0)
    w_gate = noise(seeds[3], (EXPERTS, H, D), D ** -0.5, 0.125, ((0, 16),))
    w_up = noise(seeds[4], (EXPERTS, H, D), D ** -0.5, 0.125, ((0, 16),))
    w_down = noise(seeds[5], (EXPERTS, H, D), H ** -0.5, 0.15625, ((0, 16),))
    out_grad = noise(seeds[6], (TOKENS, D), 1.0, 6.0, ((0, 32),))
    return dict(tokens=tokens, expert_ids=expert_ids, route_weights=route_weights, w_gate=w_gate, w_up=w_up, w_down=w_down, out_grad=out_grad)


def build_slots(block_ids, capacity, experts):
    onehot = (block_ids[:, None] == jnp.arange(experts, dtype=jnp.int32)[None, :]).astype(jnp.int32)
    before = jnp.cumsum(onehot, axis=0) - onehot
    position = jnp.sum(before * onehot, axis=1).astype(jnp.int32)
    slot_index = (block_ids * capacity + position).astype(jnp.int32)
    count = block_ids.shape[0]
    lookup = jnp.full((experts * capacity,), -1, jnp.int32).at[slot_index].set(jnp.arange(count, dtype=jnp.int32))
    return slot_index, lookup


def rounded(value):
    return lax.optimization_barrier(value.astype(jnp.bfloat16)).astype(jnp.float32)


def group_sum(left, right):
    rows = left.shape[0]
    left_groups = left.astype(jnp.float32).reshape(N_DP, rows // N_DP, left.shape[1])
    right_groups = right.astype(jnp.float32).reshape(N_DP, rows // N_DP, right.shape[1])
    terms = jnp.einsum("grd,grh->gdh", left_groups, right_groups)
    return jnp.sum(rounded(terms), axis=0).astype(jnp.bfloat16)


def reference(tokens, expert_ids, route_weights, w_gate, w_up, w_down, out_grad):
    blocks = N_DP * N_EXPERT
    pairs = TOK_DEV * TOPK
    block_width = H // N_TENSOR
    grouped = expert_ids.reshape(blocks, pairs).astype(jnp.int32)
    unused, lookup = jax.vmap(lambda ids: build_slots(ids, CAP, EXPERTS))(grouped)
    base = (jnp.arange(blocks, dtype=jnp.int32) * pairs)[:, None]
    flat_weights = route_weights.reshape(-1)

    def per_expert(carry, expert):
        out_total, grad_total, dot_total = carry
        local = lax.dynamic_slice_in_dim(lookup, expert * CAP, CAP, axis=1)
        filled = (local >= 0).reshape(-1)
        pair_index = jnp.where(local >= 0, local + base, 0).reshape(-1).astype(jnp.int32)
        token_index = (pair_index // TOPK).astype(jnp.int32)
        rows_in = jnp.where(filled[:, None], tokens[token_index], jnp.zeros((), tokens.dtype))
        slot_weight = jnp.where(filled, flat_weights[pair_index], jnp.zeros((), flat_weights.dtype))
        cotangent = out_grad[token_index].astype(jnp.float32)
        scaled = (slot_weight[:, None] * cotangent).astype(jnp.bfloat16)
        gate_matrix = w_gate[expert]
        up_matrix = w_up[expert]
        down_matrix = w_down[expert]
        count = rows_in.shape[0]
        gate_value = jnp.dot(rows_in, gate_matrix.T, preferred_element_type=jnp.float32)
        up_value = jnp.dot(rows_in, up_matrix.T, preferred_element_type=jnp.float32)
        hidden = (jax.nn.silu(gate_value) * up_value).astype(jnp.bfloat16)
        part = jnp.einsum("rbh,bhd->rbd", hidden.astype(jnp.float32).reshape(count, N_TENSOR, block_width),
                          down_matrix.astype(jnp.float32).reshape(N_TENSOR, block_width, D))
        summed = jnp.sum(rounded(part), axis=1)
        out_total = out_total.at[token_index].add(slot_weight[:, None] * summed)
        dots = jnp.where(filled, jnp.sum(cotangent * summed, axis=1), jnp.zeros((), jnp.float32))
        dot_total = dot_total.at[pair_index].add(dots)
        grad_hidden = jnp.dot(scaled, down_matrix.T, preferred_element_type=jnp.float32)
        sigma = jax.nn.sigmoid(gate_value)
        gate_rows = (grad_hidden * up_value * sigma * (1.0 + gate_value * (1.0 - sigma))).astype(jnp.bfloat16)
        up_rows = (grad_hidden * jax.nn.silu(gate_value)).astype(jnp.bfloat16)
        grad_part = jnp.einsum("rbh,bhd->rbd", gate_rows.astype(jnp.float32).reshape(count, N_TENSOR, block_width),
                               gate_matrix.astype(jnp.float32).reshape(N_TENSOR, block_width, D))
        grad_part = grad_part + jnp.einsum("rbh,bhd->rbd", up_rows.astype(jnp.float32).reshape(count, N_TENSOR, block_width),
                                           up_matrix.astype(jnp.float32).reshape(N_TENSOR, block_width, D))
        grad_total = grad_total.at[token_index].add(jnp.sum(rounded(grad_part), axis=1))
        gate_grad = group_sum(gate_rows, rows_in)
        up_grad = group_sum(up_rows, rows_in)
        down_grad = group_sum(hidden, scaled)
        return (out_total, grad_total, dot_total), (gate_grad, up_grad, down_grad)

    start = (jnp.zeros((TOKENS, D), jnp.float32), jnp.zeros((TOKENS, D), jnp.float32),
             jnp.zeros((TOKENS * TOPK,), jnp.float32))
    final, grads = lax.scan(per_expert, start, jnp.arange(EXPERTS, dtype=jnp.int32))
    out_total, grad_total, dot_total = final
    return (out_total.astype(jnp.bfloat16), grad_total.astype(jnp.bfloat16),
            dot_total.reshape(TOKENS, TOPK), grads[0], grads[1], grads[2])
```

```python
import jax
import jax.numpy as jnp
from jax import lax
from jax.sharding import PartitionSpec as P


def contract_rows(left, right):
    return lax.dot_general(
        left, right, (((0,), (0,)), ((), ())), preferred_element_type=jnp.float32
    )


def contract_cols(left, right):
    return lax.dot_general(
        left, right, (((1,), (1,)), ((), ())), preferred_element_type=jnp.float32
    )


def exchange(rows):
    return lax.all_to_all(rows, "expert", split_axis=0, concat_axis=0, tiled=True)


def gather_features(rows):
    if lax.axis_size("tensor") == 1:
        return rows
    return lax.all_gather(rows, "tensor", axis=1, tiled=True)


def scatter_features(rows):
    if lax.axis_size("tensor") == 1:
        return rows
    return lax.psum_scatter(rows, "tensor", scatter_dimension=1, tiled=True)


def add_other_batch(term):
    count = lax.axis_size("dp")
    total = term.astype(jnp.float32)
    moved = term
    for _ in range(count - 1):
        moved = lax.ppermute(moved, "dp", [(i, (i + 1) % count) for i in range(count)])
        total = total + moved.astype(jnp.float32)
    return total.astype(jnp.bfloat16)[None]


def body(tokens, expert_ids, route_weights, w_gate, w_up, w_down, out_grad):
    experts = lax.axis_size("expert")
    tok_rows, choose = expert_ids.shape
    capacity = tok_rows * 8 // experts
    slots = experts * capacity

    named = (expert_ids[:, :, None] == jnp.arange(experts, dtype=jnp.int32)).astype(jnp.float32)
    member = jnp.sum(named, axis=1)
    weight = jnp.sum(named * route_weights[:, :, None], axis=1)
    earlier = (
        jnp.arange(tok_rows)[:, None] > jnp.arange(tok_rows)[None, :]
    ).astype(jnp.bfloat16)
    position = jnp.dot(earlier, member.astype(jnp.bfloat16), preferred_element_type=jnp.float32)
    place = jnp.where(member > 0, position, -1.0)
    hit = place[:, :, None] == jnp.arange(capacity, dtype=jnp.float32)
    select = hit.reshape(tok_rows, slots).astype(jnp.bfloat16)
    spread = jnp.where(hit, weight[:, :, None], 0.0).reshape(tok_rows, slots)
    slot_weight = jnp.sum(spread, axis=0)
    coarse = spread.astype(jnp.bfloat16)
    fine = (spread - coarse.astype(jnp.float32)).astype(jnp.bfloat16)

    full_tokens = gather_features(tokens)
    full_grads = gather_features(out_grad)
    sent_rows = contract_rows(select, full_tokens).astype(jnp.bfloat16)
    expert_rows = exchange(sent_rows)
    sent_grads = (slot_weight[:, None] * contract_rows(select, full_grads)).astype(jnp.bfloat16)
    expert_rows, sent_grads = lax.optimization_barrier((expert_rows, sent_grads))
    expert_grads = exchange(sent_grads)

    gate_matrix = w_gate[0]
    up_matrix = w_up[0]
    down_matrix = w_down[0]
    gate_value = contract_cols(expert_rows, gate_matrix)
    up_value = contract_cols(expert_rows, up_matrix)
    sigma = jax.nn.sigmoid(gate_value)
    silu = gate_value * sigma
    hidden = (silu * up_value).astype(jnp.bfloat16)
    part = jnp.dot(hidden, down_matrix, preferred_element_type=jnp.float32).astype(jnp.bfloat16)
    part, expert_grads = lax.optimization_barrier((part, expert_grads))
    returned = exchange(scatter_features(part))

    grad_hidden = contract_cols(expert_grads, down_matrix)
    gate_rows = (grad_hidden * up_value * sigma * (1.0 + gate_value * (1.0 - sigma))).astype(
        jnp.bfloat16
    )
    up_rows = (grad_hidden * silu).astype(jnp.bfloat16)
    down_term = contract_rows(hidden, expert_grads).astype(jnp.bfloat16)
    gate_term = contract_rows(gate_rows, expert_rows).astype(jnp.bfloat16)
    up_term = contract_rows(up_rows, expert_rows).astype(jnp.bfloat16)
    gate_rows, up_rows, down_term, gate_term, up_term = lax.optimization_barrier(
        (gate_rows, up_rows, down_term, gate_term, up_term)
    )
    down_out = add_other_batch(down_term)
    gate_out = add_other_batch(gate_term)
    up_out = add_other_batch(up_term)
    grad_part = (
        jnp.dot(gate_rows, gate_matrix, preferred_element_type=jnp.float32)
        + jnp.dot(up_rows, up_matrix, preferred_element_type=jnp.float32)
    ).astype(jnp.bfloat16)
    grad_part, returned = lax.optimization_barrier((grad_part, returned))
    returned_grads = exchange(scatter_features(grad_part))

    layer_out = (
        jnp.dot(coarse, returned, preferred_element_type=jnp.float32)
        + jnp.dot(fine, returned, preferred_element_type=jnp.float32)
    ).astype(jnp.bfloat16)
    products = contract_cols(out_grad, returned).reshape(tok_rows, experts, capacity)
    dots = jnp.sum(jnp.where(hit, products, 0.0), axis=2)
    weight_dots = jnp.sum(named * dots[:, None, :], axis=2)
    if lax.axis_size("tensor") > 1:
        weight_dots = lax.psum(weight_dots, "tensor")
    grad_tokens = jnp.dot(select, returned_grads, preferred_element_type=jnp.float32).astype(
        jnp.bfloat16
    )
    return (layer_out, grad_tokens, weight_dots, gate_out, up_out, down_out)


def solution(mesh):
    placed = (
        P(("dp", "expert"), "tensor"),
        P(("dp", "expert"), None),
        P(("dp", "expert"), None),
        P("expert", "tensor", None),
        P("expert", "tensor", None),
        P("expert", "tensor", None),
        P(("dp", "expert"), "tensor"),
    )
    return jax.shard_map(
        body,
        mesh=mesh,
        in_specs=placed,
        out_specs=(
            P(("dp", "expert"), "tensor"),
            P(("dp", "expert"), "tensor"),
            P(("dp", "expert"), None),
            P("expert", "tensor", None),
            P("expert", "tensor", None),
            P("expert", "tensor", None),
        ),
        check_vma=False,
    )
```

```python
import functools
import jax
import jax.numpy as jnp
from jax import lax
from jax.experimental import pallas as pl
from jax.experimental.pallas import tpu as pltpu
from jax.sharding import PartitionSpec as P


def contract_rows(left, right):
    return lax.dot_general(
        left, right, (((0,), (0,)), ((), ())), preferred_element_type=jnp.float32
    )


def contract_cols(left, right):
    return lax.dot_general(
        left, right, (((1,), (1,)), ((), ())), preferred_element_type=jnp.float32
    )


def exchange(rows):
    return lax.all_to_all(rows, "expert", split_axis=0, concat_axis=0, tiled=True)


def gather_features(rows):
    if lax.axis_size("tensor") == 1:
        return rows
    return lax.all_gather(rows, "tensor", axis=1, tiled=True)


def scatter_features(rows):
    if lax.axis_size("tensor") == 1:
        return rows
    return lax.psum_scatter(rows, "tensor", scatter_dimension=1, tiled=True)


def add_other_batch(term):
    count = lax.axis_size("dp")
    total = term.astype(jnp.float32)
    moved = term
    for _ in range(count - 1):
        moved = lax.ppermute(moved, "dp", [(i, (i + 1) % count) for i in range(count)])
        total = total + moved.astype(jnp.float32)
    return total.astype(jnp.bfloat16)[None]


def dispatch_kernel(outer, inner, capacity, x_ref, g_ref, p_ref, rows_ref, grads_ref,
                    far_x, far_g, far_p, own_x, own_g, far_send, far_recv, near_send, near_recv):
    me = lax.axis_index("expert")
    plane, spot = me // inner, me % inner

    def far_id(step):
        return {"expert": ((plane + step) % outer) * inner + spot}

    def near_id(step):
        return {"expert": plane * inner + (spot + step) % inner}

    barrier = pltpu.get_barrier_semaphore()
    for step in range(1, outer):
        pl.semaphore_signal(barrier, inc=1, device_id=far_id(step), device_id_type=pl.DeviceIdType.MESH)
    for step in range(1, inner):
        pl.semaphore_signal(barrier, inc=1, device_id=near_id(step), device_id_type=pl.DeviceIdType.MESH)
    pl.semaphore_wait(barrier, outer + inner - 2)

    def far_copy(step, kind):
        source = (x_ref, p_ref.at[(plane + step) % outer], g_ref)[kind]
        landing = (far_x, far_p, far_g)[kind]
        return pltpu.make_async_remote_copy(
            src_ref=source,
            dst_ref=landing.at[step - 1],
            send_sem=far_send.at[step - 1, kind],
            recv_sem=far_recv.at[step - 1, kind],
            device_id=far_id(step),
            device_id_type=pl.DeviceIdType.MESH,
        )

    def near_copy(block, step, kind):
        source = (own_x, own_g)[kind]
        landing = (rows_ref, grads_ref)[kind]
        start = pl.multiple_of(((spot + step) % inner) * capacity, capacity)
        origin = (plane + outer - block) % outer
        place = pl.multiple_of((origin * inner + spot) * capacity, capacity)
        return pltpu.make_async_remote_copy(
            src_ref=source.at[block, pl.ds(start, capacity)],
            dst_ref=landing.at[pl.ds(place, capacity)],
            send_sem=near_send.at[block, step - 1, kind],
            recv_sem=near_recv.at[block, step - 1, kind],
            device_id=near_id(step),
            device_id_type=pl.DeviceIdType.MESH,
        )

    for kind in range(3):
        for step in range(1, outer):
            far_copy(step, kind).start()

    def choose(block, kind):
        if block == 0:
            picks = p_ref[plane]
            values = (x_ref, g_ref)[kind][...]
        else:
            if kind == 0:
                far_copy(block, 0).wait_recv()
                far_copy(block, 1).wait_recv()
            else:
                far_copy(block, 2).wait_recv()
            picks = far_p[block - 1]
            values = (far_x, far_g)[kind][block - 1]
        if kind == 0:
            lane = lax.broadcasted_iota(jnp.int32, picks.shape, 1)
            taken = (picks.astype(jnp.float32) > 0.0) & (lane < values.shape[0])
            picks = jnp.where(taken, 1.0, 0.0).astype(jnp.bfloat16)
        twice = jnp.concatenate([values, values], axis=0)
        chosen = jnp.dot(picks, twice, preferred_element_type=jnp.float32).astype(jnp.bfloat16)
        kept = (own_x, own_g)[kind]
        kept[block] = chosen
        for step in range(1, inner):
            near_copy(block, step, kind).start()
        origin = (plane + outer - block) % outer
        place = pl.multiple_of((origin * inner + spot) * capacity, capacity)
        start = pl.multiple_of(spot * capacity, capacity)
        landing = (rows_ref, grads_ref)[kind]
        landing[pl.ds(place, capacity)] = kept[block, pl.ds(start, capacity)]

    choose(0, 0)
    choose(0, 1)
    for kind in range(2):
        for block in range(1, outer):
            choose(block, kind)
    for kind in range(3):
        for step in range(1, outer):
            far_copy(step, kind).wait_send()
    for kind in range(2):
        for block in range(outer):
            for step in range(1, inner):
                near_copy(block, step, kind).wait()


def dispatch(tokens, grads, picks, outer, inner, capacity):
    rows, width = tokens.shape
    slots = outer * inner * capacity
    bf16 = jnp.bfloat16
    landed = jax.ShapeDtypeStruct((slots, width), bf16)
    return pl.pallas_call(
        functools.partial(dispatch_kernel, outer, inner, capacity),
        out_shape=(landed, landed),
        in_specs=[pl.BlockSpec(memory_space=pltpu.VMEM)] * 3,
        out_specs=[pl.BlockSpec(memory_space=pltpu.VMEM)] * 2,
        scratch_shapes=[
            pltpu.VMEM((outer - 1, rows, width), bf16),
            pltpu.VMEM((outer - 1, rows, width), bf16),
            pltpu.VMEM((outer - 1, inner * capacity, 2 * rows), bf16),
            pltpu.VMEM((outer, inner * capacity, width), bf16),
            pltpu.VMEM((outer, inner * capacity, width), bf16),
            pltpu.SemaphoreType.DMA((outer - 1, 3)),
            pltpu.SemaphoreType.DMA((outer - 1, 3)),
            pltpu.SemaphoreType.DMA((outer, inner - 1, 2)),
            pltpu.SemaphoreType.DMA((outer, inner - 1, 2)),
        ],
        compiler_params=pltpu.CompilerParams(
            collective_id=0, has_side_effects=True, vmem_limit_bytes=32 * 1024 * 1024
        ),
    )(tokens, grads, picks)


def body(tokens, expert_ids, route_weights, w_gate, w_up, w_down, out_grad):
    experts = lax.axis_size("expert")
    tok_rows, choose = expert_ids.shape
    capacity = tok_rows * 8 // experts
    slots = experts * capacity

    named = (expert_ids[:, :, None] == jnp.arange(experts, dtype=jnp.int32)).astype(jnp.float32)
    member = jnp.sum(named, axis=1)
    weight = jnp.sum(named * route_weights[:, :, None], axis=1)
    earlier = (
        jnp.arange(tok_rows)[:, None] > jnp.arange(tok_rows)[None, :]
    ).astype(jnp.bfloat16)
    position = jnp.dot(earlier, member.astype(jnp.bfloat16), preferred_element_type=jnp.float32)
    place = jnp.where(member > 0, position, -1.0)
    hit = place[:, :, None] == jnp.arange(capacity, dtype=jnp.float32)
    select = hit.reshape(tok_rows, slots).astype(jnp.bfloat16)
    spread = jnp.where(hit, weight[:, :, None], 0.0).reshape(tok_rows, slots)
    coarse = spread.astype(jnp.bfloat16)
    fine = (spread - coarse.astype(jnp.float32)).astype(jnp.bfloat16)

    full_tokens = gather_features(tokens)
    full_grads = gather_features(out_grad)
    inner = 4
    outer = experts // inner
    picks = jnp.concatenate([coarse, fine], axis=0).T.reshape(outer, inner * capacity, 2 * tok_rows)
    expert_rows, expert_grads = dispatch(full_tokens, full_grads, picks, outer, inner, capacity)

    gate_matrix = w_gate[0]
    up_matrix = w_up[0]
    down_matrix = w_down[0]
    gate_value = contract_cols(expert_rows, gate_matrix)
    up_value = contract_cols(expert_rows, up_matrix)
    sigma = jax.nn.sigmoid(gate_value)
    silu = gate_value * sigma
    hidden = (silu * up_value).astype(jnp.bfloat16)
    part = jnp.dot(hidden, down_matrix, preferred_element_type=jnp.float32).astype(jnp.bfloat16)
    part, expert_grads = lax.optimization_barrier((part, expert_grads))
    returned = exchange(scatter_features(part))

    grad_hidden = contract_cols(expert_grads, down_matrix)
    gate_rows = (grad_hidden * up_value * sigma * (1.0 + gate_value * (1.0 - sigma))).astype(
        jnp.bfloat16
    )
    up_rows = (grad_hidden * silu).astype(jnp.bfloat16)
    down_term = contract_rows(hidden, expert_grads).astype(jnp.bfloat16)
    gate_term = contract_rows(gate_rows, expert_rows).astype(jnp.bfloat16)
    up_term = contract_rows(up_rows, expert_rows).astype(jnp.bfloat16)
    gate_rows, up_rows, down_term, gate_term, up_term, returned = lax.optimization_barrier(
        (gate_rows, up_rows, down_term, gate_term, up_term, returned)
    )
    down_out = add_other_batch(down_term)
    gate_out = add_other_batch(gate_term)
    up_out = add_other_batch(up_term)
    grad_part = (
        jnp.dot(gate_rows, gate_matrix, preferred_element_type=jnp.float32)
        + jnp.dot(up_rows, up_matrix, preferred_element_type=jnp.float32)
    ).astype(jnp.bfloat16)
    returned_grads = exchange(scatter_features(grad_part))

    layer_out = (
        jnp.dot(coarse, returned, preferred_element_type=jnp.float32)
        + jnp.dot(fine, returned, preferred_element_type=jnp.float32)
    ).astype(jnp.bfloat16)
    products = contract_cols(out_grad, returned).reshape(tok_rows, experts, capacity)
    dots = jnp.sum(jnp.where(hit, products, 0.0), axis=2)
    weight_dots = jnp.sum(named * dots[:, None, :], axis=2)
    if lax.axis_size("tensor") > 1:
        weight_dots = lax.psum(weight_dots, "tensor")
    returned_grads, gate_out, up_out, down_out = lax.optimization_barrier(
        (returned_grads, gate_out, up_out, down_out)
    )
    grad_tokens = jnp.dot(select, returned_grads, preferred_element_type=jnp.float32).astype(
        jnp.bfloat16
    )
    return (layer_out, grad_tokens, weight_dots, gate_out, up_out, down_out)


def solution(mesh):
    placed = (
        P(("dp", "expert"), "tensor"),
        P(("dp", "expert"), None),
        P(("dp", "expert"), None),
        P("expert", "tensor", None),
        P("expert", "tensor", None),
        P("expert", "tensor", None),
        P(("dp", "expert"), "tensor"),
    )
    return jax.shard_map(
        body,
        mesh=mesh,
        in_specs=placed,
        out_specs=(
            P(("dp", "expert"), "tensor"),
            P(("dp", "expert"), "tensor"),
            P(("dp", "expert"), None),
            P("expert", "tensor", None),
            P("expert", "tensor", None),
            P("expert", "tensor", None),
        ),
        check_vma=False,
    )
```

```python
import functools
import jax
import jax.numpy as jnp
from jax import lax
from jax.experimental import pallas as pl
from jax.experimental.pallas import tpu as pltpu
from jax.sharding import PartitionSpec as P


def contract_rows(left, right):
    return lax.dot_general(
        left, right, (((0,), (0,)), ((), ())), preferred_element_type=jnp.float32
    )


def contract_cols(left, right):
    return lax.dot_general(
        left, right, (((1,), (1,)), ((), ())), preferred_element_type=jnp.float32
    )


def exchange(rows):
    return lax.all_to_all(rows, "expert", split_axis=0, concat_axis=0, tiled=True)


def gather_features(rows):
    if lax.axis_size("tensor") == 1:
        return rows
    return lax.all_gather(rows, "tensor", axis=1, tiled=True)


def scatter_features(rows):
    if lax.axis_size("tensor") == 1:
        return rows
    return lax.psum_scatter(rows, "tensor", scatter_dimension=1, tiled=True)


def add_other_batch(term):
    count = lax.axis_size("dp")
    total = term.astype(jnp.float32)
    moved = term
    for _ in range(count - 1):
        moved = lax.ppermute(moved, "dp", [(i, (i + 1) % count) for i in range(count)])
        total = total + moved.astype(jnp.float32)
    return total.astype(jnp.bfloat16)[None]


def dispatch_kernel(outer, inner, capacity, x_ref, g_ref, p_ref, rows_ref, grads_ref,
                    far_x, far_g, far_p, own_x, own_g, far_send, far_recv, near_send, near_recv):
    me = lax.axis_index("expert")
    plane, spot = me // inner, me % inner

    def far_id(step):
        return {"expert": ((plane + step) % outer) * inner + spot}

    def near_id(step):
        return {"expert": plane * inner + (spot + step) % inner}

    barrier = pltpu.get_barrier_semaphore()
    for step in range(1, outer):
        pl.semaphore_signal(barrier, inc=1, device_id=far_id(step), device_id_type=pl.DeviceIdType.MESH)
    for step in range(1, inner):
        pl.semaphore_signal(barrier, inc=1, device_id=near_id(step), device_id_type=pl.DeviceIdType.MESH)
    pl.semaphore_wait(barrier, outer + inner - 2)

    def far_copy(step, kind):
        source = (x_ref, p_ref.at[(plane + step) % outer], g_ref)[kind]
        landing = (far_x, far_p, far_g)[kind]
        return pltpu.make_async_remote_copy(
            src_ref=source,
            dst_ref=landing.at[step - 1],
            send_sem=far_send.at[step - 1, kind],
            recv_sem=far_recv.at[step - 1, kind],
            device_id=far_id(step),
            device_id_type=pl.DeviceIdType.MESH,
        )

    def near_copy(block, step, kind):
        source = (own_x, own_g)[kind]
        landing = (rows_ref, grads_ref)[kind]
        start = pl.multiple_of(((spot + step) % inner) * capacity, capacity)
        origin = (plane + outer - block) % outer
        place = pl.multiple_of((origin * inner + spot) * capacity, capacity)
        return pltpu.make_async_remote_copy(
            src_ref=source.at[block, pl.ds(start, capacity)],
            dst_ref=landing.at[pl.ds(place, capacity)],
            send_sem=near_send.at[block, step - 1, kind],
            recv_sem=near_recv.at[block, step - 1, kind],
            device_id=near_id(step),
            device_id_type=pl.DeviceIdType.MESH,
        )

    for kind in range(3):
        for step in range(1, outer):
            far_copy(step, kind).start()

    def choose(block, kind):
        if block == 0:
            picks = p_ref[plane]
            values = (x_ref, g_ref)[kind][...]
        else:
            if kind == 0:
                far_copy(block, 0).wait_recv()
                far_copy(block, 1).wait_recv()
            else:
                far_copy(block, 2).wait_recv()
            picks = far_p[block - 1]
            values = (far_x, far_g)[kind][block - 1]
        if kind == 0:
            lane = lax.broadcasted_iota(jnp.int32, picks.shape, 1)
            taken = (picks.astype(jnp.float32) > 0.0) & (lane < values.shape[0])
            picks = jnp.where(taken, 1.0, 0.0).astype(jnp.bfloat16)
        twice = jnp.concatenate([values, values], axis=0)
        chosen = jnp.dot(picks, twice, preferred_element_type=jnp.float32).astype(jnp.bfloat16)
        kept = (own_x, own_g)[kind]
        kept[block] = chosen
        for step in range(1, inner):
            near_copy(block, step, kind).start()
        origin = (plane + outer - block) % outer
        place = pl.multiple_of((origin * inner + spot) * capacity, capacity)
        start = pl.multiple_of(spot * capacity, capacity)
        landing = (rows_ref, grads_ref)[kind]
        landing[pl.ds(place, capacity)] = kept[block, pl.ds(start, capacity)]

    choose(0, 0)
    choose(0, 1)
    for kind in range(2):
        for block in range(1, outer):
            choose(block, kind)
    for kind in range(3):
        for step in range(1, outer):
            far_copy(step, kind).wait_send()
    for kind in range(2):
        for block in range(outer):
            for step in range(1, inner):
                near_copy(block, step, kind).wait()


def dispatch(tokens, grads, picks, outer, inner, capacity):
    rows, width = tokens.shape
    slots = outer * inner * capacity
    bf16 = jnp.bfloat16
    landed = jax.ShapeDtypeStruct((slots, width), bf16)
    return pl.pallas_call(
        functools.partial(dispatch_kernel, outer, inner, capacity),
        out_shape=(landed, landed),
        in_specs=[pl.BlockSpec(memory_space=pltpu.VMEM)] * 3,
        out_specs=[pl.BlockSpec(memory_space=pltpu.VMEM)] * 2,
        scratch_shapes=[
            pltpu.VMEM((outer - 1, rows, width), bf16),
            pltpu.VMEM((outer - 1, rows, width), bf16),
            pltpu.VMEM((outer - 1, inner * capacity, 2 * rows), bf16),
            pltpu.VMEM((outer, inner * capacity, width), bf16),
            pltpu.VMEM((outer, inner * capacity, width), bf16),
            pltpu.SemaphoreType.DMA((outer - 1, 3)),
            pltpu.SemaphoreType.DMA((outer - 1, 3)),
            pltpu.SemaphoreType.DMA((outer, inner - 1, 2)),
            pltpu.SemaphoreType.DMA((outer, inner - 1, 2)),
        ],
        compiler_params=pltpu.CompilerParams(
            collective_id=0, has_side_effects=True, vmem_limit_bytes=32 * 1024 * 1024
        ),
    )(tokens, grads, picks)


def body(tokens, expert_ids, route_weights, w_gate, w_up, w_down, out_grad):
    experts = lax.axis_size("expert")
    tok_rows, choose = expert_ids.shape
    capacity = tok_rows * 8 // experts
    slots = experts * capacity

    named = (expert_ids[:, :, None] == jnp.arange(experts, dtype=jnp.int32)).astype(jnp.float32)
    member = jnp.sum(named, axis=1)
    weight = jnp.sum(named * route_weights[:, :, None], axis=1)
    earlier = (
        jnp.arange(tok_rows)[:, None] > jnp.arange(tok_rows)[None, :]
    ).astype(jnp.bfloat16)
    position = jnp.dot(earlier, member.astype(jnp.bfloat16), preferred_element_type=jnp.float32)
    place = jnp.where(member > 0, position, -1.0)
    hit = place[:, :, None] == jnp.arange(capacity, dtype=jnp.float32)
    select = hit.reshape(tok_rows, slots).astype(jnp.bfloat16)
    spread = jnp.where(hit, weight[:, :, None], 0.0).reshape(tok_rows, slots)
    coarse = spread.astype(jnp.bfloat16)
    fine = (spread - coarse.astype(jnp.float32)).astype(jnp.bfloat16)

    full_tokens = gather_features(tokens)
    full_grads = gather_features(out_grad)
    inner = 4
    outer = experts // inner
    picks = jnp.concatenate([coarse, fine], axis=0).T.reshape(outer, inner * capacity, 2 * tok_rows)
    expert_rows, expert_grads = dispatch(full_tokens, full_grads, picks, outer, inner, capacity)

    gate_matrix = w_gate[0]
    up_matrix = w_up[0]
    down_matrix = w_down[0]
    gate_value = contract_cols(expert_rows, gate_matrix)
    up_value = contract_cols(expert_rows, up_matrix)
    sigma = jax.nn.sigmoid(gate_value)
    silu = gate_value * sigma
    hidden = (silu * up_value).astype(jnp.bfloat16)
    part = jnp.dot(hidden, down_matrix, preferred_element_type=jnp.float32).astype(jnp.bfloat16)
    part, expert_grads = lax.optimization_barrier((part, expert_grads))
    returned = exchange(scatter_features(part))

    grad_hidden = contract_cols(expert_grads, down_matrix)
    gate_rows = (grad_hidden * up_value * sigma * (1.0 + gate_value * (1.0 - sigma))).astype(
        jnp.bfloat16
    )
    up_rows = (grad_hidden * silu).astype(jnp.bfloat16)
    down_term = contract_rows(hidden, expert_grads).astype(jnp.bfloat16)
    gate_term = contract_rows(gate_rows, expert_rows).astype(jnp.bfloat16)
    up_term = contract_rows(up_rows, expert_rows).astype(jnp.bfloat16)
    gate_share = jnp.dot(gate_rows, gate_matrix, preferred_element_type=jnp.float32)
    gate_share, up_rows, down_term, gate_term, up_term, returned = lax.optimization_barrier(
        (gate_share, up_rows, down_term, gate_term, up_term, returned)
    )
    down_out = add_other_batch(down_term)
    gate_out = add_other_batch(gate_term)
    up_out = add_other_batch(up_term)
    grad_part = (
        gate_share
        + jnp.dot(up_rows, up_matrix, preferred_element_type=jnp.float32)
    ).astype(jnp.bfloat16)
    returned_grads = exchange(scatter_features(grad_part))

    layer_out = (
        jnp.dot(coarse, returned, preferred_element_type=jnp.float32)
        + jnp.dot(fine, returned, preferred_element_type=jnp.float32)
    ).astype(jnp.bfloat16)
    products = contract_cols(out_grad, returned).reshape(tok_rows, experts, capacity)
    dots = jnp.sum(jnp.where(hit, products, 0.0), axis=2)
    weight_dots = jnp.sum(named * dots[:, None, :], axis=2)
    if lax.axis_size("tensor") > 1:
        weight_dots = lax.psum(weight_dots, "tensor")
    returned_grads, gate_out, up_out, down_out = lax.optimization_barrier(
        (returned_grads, gate_out, up_out, down_out)
    )
    grad_tokens = jnp.dot(select, returned_grads, preferred_element_type=jnp.float32).astype(
        jnp.bfloat16
    )
    return (layer_out, grad_tokens, weight_dots, gate_out, up_out, down_out)


def solution(mesh):
    placed = (
        P(("dp", "expert"), "tensor"),
        P(("dp", "expert"), None),
        P(("dp", "expert"), None),
        P("expert", "tensor", None),
        P("expert", "tensor", None),
        P("expert", "tensor", None),
        P(("dp", "expert"), "tensor"),
    )
    return jax.shard_map(
        body,
        mesh=mesh,
        in_specs=placed,
        out_specs=(
            P(("dp", "expert"), "tensor"),
            P(("dp", "expert"), "tensor"),
            P(("dp", "expert"), None),
            P("expert", "tensor", None),
            P("expert", "tensor", None),
            P("expert", "tensor", None),
        ),
        check_vma=False,
    )
```
